32 devices in a mesh: layer: 8 (over z, core), row: 4 (over y, x).
Axes of the slice: x: 2, y: 2, z: 4, core: 2. Of those that a mesh axis runs over, the one named last changes fastest.
Arguments:
- propagator: float32 [8, 16384, 6, 128], P('layer', 'row'), may hold values from -0.15625 to 0.15625
- col_blocks: int32 [8, 128, 6], P('layer', 'row'), may hold values from 0 to 127, as said below
- sources: bfloat16 [8, 8, 56, 16384], P(None, 'layer', None, 'row'), may hold values from -6 to 6
- incoming: bfloat16 [8, 56, 16384], P('layer', None, 'row'), may hold values from -6 to 6
Outputs:
- outgoing: bfloat16 [8, 8, 56, 16384], P(None, 'layer', None, 'row')
The draws below stay inside these ranges and needn't reach their ends.
Inputs may be any that keep to these rules, and one draw needn't show every extreme that they name: col_blocks[l, r, k] differs from r by at most 32; slot 0 is r itself, slots 1 and 2 are r - 32 and r + 32 kept within 0 .. 127; entries of one row block may repeat.
All inputs are finite; a program needn't handle non-finite values.
Results may differ from the reference program's by a relative error of at most 0.0043.
Values may be sent and summed in bfloat16 or wider, within the bound.
No kernel may reach another device: no remote copies, remote signals or barrier semaphores. Data moves between devices by JAX's collectives and lax.ppermute only.
A program may use at most 64 MiB of HBM per device.

```python
import jax
import jax.numpy as jnp
from jax import lax

M = 16384
BLK = 128
NBLK = 6
SHOTS = 56
TICKS = 8
LAYERS = 8
RB = 128
RBD = 32


def draw_col_blocks(key, part):
    row_ids = jnp.arange(RB, dtype=jnp.int32)[None, :, None]
    slot_ids = jnp.arange(NBLK, dtype=jnp.int32)[None, None, :]
    offsets = jax.random.randint(key, (LAYERS, RB, NBLK), -RBD, RBD + 1, dtype=jnp.int32)
    offsets = jnp.where(slot_ids == 0, 0, jnp.where(slot_ids == 1, -RBD, jnp.where(slot_ids == 2, RBD, offsets)))
    return jnp.clip(row_ids + offsets, 0, RB - 1).astype(jnp.int32)


def levels(rng, extent, shards, smallest, largest):
    gain = 1.0
    for dim, blocks in shards:
        steps = jax.random.uniform(jax.random.fold_in(jax.random.fold_in(rng, 6), dim), (blocks,), jnp.float32, smallest / len(shards), largest / len(shards))
        gain = gain * jnp.repeat(jnp.exp(steps), extent[dim] // blocks).reshape((-1,) + (1,) * (len(extent) - 1 - dim))
    return gain


def centred(own_key, extent, scale, bound, cuts=(), held_as=jnp.bfloat16):
    factor_of = levels(own_key, extent, cuts, -0.22, 0.18) if cuts else 1.0
    values = jax.random.normal(own_key, extent, jnp.float32) * scale * factor_of
    return jnp.minimum(jnp.maximum(values, -bound), bound).astype(held_as)


def setup_inputs(seed: int = 0) -> dict:
    splits = jax.random.split(jax.random.key(seed), 5)
    propagator = centred(splits[0], (LAYERS, M, NBLK, BLK), (2 * NBLK * BLK) ** -0.5, 0.15625, ((0, 8), (1, 4)), jnp.float32)
    col_blocks = draw_col_blocks(jax.random.fold_in(splits[4], 71), 0)
    sources = centred(splits[2], (TICKS, LAYERS, SHOTS, M), 1.0, 6.0, ((1, 8), (3, 4)))
    incoming = centred(splits[3], (LAYERS, SHOTS, M), 1.0, 6.0, ((0, 8), (2, 4)))
    return dict(propagator=propagator, col_blocks=col_blocks, sources=sources, incoming=incoming)


def apply_layer(layer_prop, layer_cols, arriving, layer_source):
    shot_count = arriving.shape[0]
    blocks = arriving.astype(jnp.float32).reshape(shot_count, RB, BLK)
    picked = blocks[:, layer_cols, :]
    weights = layer_prop.reshape(RB, BLK, NBLK, BLK)
    mixed_rows = jnp.einsum('srkc,rbkc->srb', picked, weights, precision=lax.Precision.HIGHEST)
    total = mixed_rows.reshape(shot_count, M) + layer_source.astype(jnp.float32)
    return total.astype(jnp.bfloat16)


def reference(propagator, col_blocks, sources, incoming):
    arriving = incoming
    history = []
    for tick_index in range(TICKS):
        produced = lax.map(lambda packed: apply_layer(packed[0], packed[1], packed[2], packed[3]),
                           (propagator, col_blocks, arriving, sources[tick_index]))
        history.append(produced)
        arriving = jnp.concatenate([jnp.zeros_like(produced[:1]), produced[:-1]], axis=0)
    return jnp.stack(history)
```

```python
import functools

import jax
import jax.numpy as jnp
from jax import lax
from jax.experimental import pallas as pl
from jax.experimental.pallas import tpu as pltpu
from jax.sharding import PartitionSpec as P

MIB = 1024 * 1024


def split_kernel(prop_ref, weights_ref):
    slots, _, blk = prop_ref.shape
    for k in range(slots):
        block = prop_ref[k].T
        high = block.astype(jnp.bfloat16)
        low = (block - high.astype(jnp.float32)).astype(jnp.bfloat16)
        weights_ref[0, k * blk:(k + 1) * blk, :blk] = high
        weights_ref[0, k * blk:(k + 1) * blk, blk:] = low


def split_weights(prop):
    slots, rows, blk = prop.shape
    return pl.pallas_call(
        split_kernel,
        grid=(rows // blk,),
        in_specs=[pl.BlockSpec((slots, blk, blk), lambda r: (0, r, 0))],
        out_specs=pl.BlockSpec((1, slots * blk, 2 * blk), lambda r: (r, 0, 0)),
        out_shape=jax.ShapeDtypeStruct((rows // blk, slots * blk, 2 * blk), jnp.bfloat16),
        name="split_weights",
    )(prop)


def tick_kernel(cols_ref, weights_ref, left_ref, own_ref, right_ref, source_ref, out_ref, window):
    width = own_ref.shape[1]
    row_blocks, depth, twice = weights_ref.shape
    blk = twice // 2
    slots = depth // blk
    window[:, :width] = left_ref[...]
    window[:, width:2 * width] = own_ref[...]
    window[:, 2 * width:] = right_ref[...]

    def step(r, carry):
        picked = []
        for k in range(slots):
            start = pl.multiple_of(cols_ref[r * slots + k] * blk, blk)
            picked.append(window[:, pl.ds(start, blk)])
        both = jnp.dot(jnp.concatenate(picked, axis=1), weights_ref[r], preferred_element_type=jnp.float32)
        here = pl.ds(pl.multiple_of(r * blk, blk), blk)
        total = both[:, :blk] + both[:, blk:] + source_ref[:, here].astype(jnp.float32)
        out_ref[:, here] = total.astype(out_ref.dtype)
        return carry

    lax.fori_loop(0, row_blocks, step, 0, unroll=4)


def apply_layer(cols, weights, left, own, right, source):
    shots, width = own.shape
    vmem = pl.BlockSpec(memory_space=pltpu.VMEM)
    return pl.pallas_call(
        tick_kernel,
        in_specs=[pl.BlockSpec(memory_space=pltpu.SMEM)] + [vmem] * 5,
        out_specs=vmem,
        out_shape=jax.ShapeDtypeStruct((shots, width), jnp.bfloat16),
        scratch_shapes=[pltpu.VMEM((shots, 3 * width), jnp.bfloat16)],
        compiler_params=pltpu.CompilerParams(vmem_limit_bytes=32 * MIB),
        cost_estimate=pl.CostEstimate(
            flops=2 * shots * weights.size, bytes_accessed=weights.size * 2, transcendentals=0
        ),
        name="apply_layer",
    )(cols, weights, left, own, right, source)


def hop(value, layers, rows, up, side):
    pairs = []
    for l in range(layers - up):
        for r in range(rows):
            if 0 <= r + side < rows:
                pairs.append((l * rows + r, (l + up) * rows + r + side))
    return lax.ppermute(value, ("layer", "row"), pairs)


def body(propagator, col_blocks, sources, incoming):
    _, row_count, slots, blk = propagator.shape
    ticks = sources.shape[0]
    layers = lax.axis_size("layer")
    rows = lax.axis_size("row")
    block_count = row_count // blk
    cols = (col_blocks[0] - (lax.axis_index("row") - 1) * block_count).reshape(-1)
    own = incoming[0]
    left = hop(own, layers, rows, 0, 1)
    right = hop(own, layers, rows, 0, -1)
    weights = split_weights(jnp.transpose(propagator[0], (1, 0, 2)))
    history = []
    for tick in range(ticks):
        produced = apply_layer(cols, weights, left, own, right, sources[tick, 0])
        history.append(produced)
        if tick + 1 < ticks:
            left = hop(produced, layers, rows, 1, 1)
            right = hop(produced, layers, rows, 1, -1)
            own = hop(produced, layers, rows, 1, 0)
    return jnp.stack(history)[:, None]


def solution(mesh):
    return jax.shard_map(
        body,
        mesh=mesh,
        in_specs=(
            P("layer", "row", None, None),
            P("layer", "row", None),
            P(None, "layer", None, "row"),
            P("layer", None, "row"),
        ),
        out_specs=P(None, "layer", None, "row"),
        check_vma=False,
    )
```

```python
import functools

import jax
import jax.numpy as jnp
from jax import lax
from jax.experimental import pallas as pl
from jax.experimental.pallas import tpu as pltpu
from jax.sharding import PartitionSpec as P

MIB = 1024 * 1024


def split_kernel(prop_ref, weights_ref):
    slots, _, blk = prop_ref.shape
    for k in range(slots):
        block = prop_ref[k]
        high = block.astype(jnp.bfloat16)
        low = (block - high.astype(jnp.float32)).astype(jnp.bfloat16)
        weights_ref[0, :blk, k * blk:(k + 1) * blk] = high
        weights_ref[0, blk:, k * blk:(k + 1) * blk] = low


def split_weights(prop):
    slots, rows, blk = prop.shape
    return pl.pallas_call(
        split_kernel,
        grid=(rows // blk,),
        in_specs=[pl.BlockSpec((slots, blk, blk), lambda r: (0, r, 0))],
        out_specs=pl.BlockSpec((1, 2 * blk, slots * blk), lambda r: (r, 0, 0)),
        out_shape=jax.ShapeDtypeStruct((rows // blk, 2 * blk, slots * blk), jnp.bfloat16),
        name="split_weights",
    )(prop)


def tick_kernel(cols_ref, weights_ref, gathered_ref, source_ref, out_ref):
    _, shots, width = gathered_ref.shape
    row_blocks, twice, depth = weights_ref.shape
    blk = twice // 2
    slots = depth // blk
    per_shard = width // blk

    def step(r, carry):
        picked = []
        for k in range(slots):
            col = cols_ref[r * slots + k]
            start = pl.multiple_of(lax.rem(col, per_shard) * blk, blk)
            picked.append(gathered_ref[lax.div(col, per_shard), :, pl.ds(start, blk)])
        both = lax.dot_general(
            jnp.concatenate(picked, axis=1),
            weights_ref[r],
            (((1,), (1,)), ((), ())),
            preferred_element_type=jnp.float32,
        )
        here = pl.ds(pl.multiple_of(r * blk, blk), blk)
        total = both[:, :blk] + both[:, blk:] + source_ref[:, here].astype(jnp.float32)
        out_ref[:, here] = total.astype(out_ref.dtype)
        return carry

    lax.fori_loop(0, row_blocks, step, 0, unroll=4)


def apply_layer(cols, weights, gathered, source):
    _, shots, width = gathered.shape
    vmem = pl.BlockSpec(memory_space=pltpu.VMEM)
    return pl.pallas_call(
        tick_kernel,
        in_specs=[pl.BlockSpec(memory_space=pltpu.SMEM)] + [vmem] * 3,
        out_specs=vmem,
        out_shape=jax.ShapeDtypeStruct((shots, width), jnp.bfloat16),
        compiler_params=pltpu.CompilerParams(vmem_limit_bytes=32 * MIB),
        cost_estimate=pl.CostEstimate(
            flops=2 * shots * weights.size, bytes_accessed=weights.size * 2, transcendentals=0
        ),
        name="apply_layer",
    )(cols, weights, gathered, source)


def hop(value, layers, rows, up, side):
    pairs = []
    for l in range(layers - up):
        for r in range(rows):
            if 0 <= r + side < rows:
                pairs.append((l * rows + r, (l + up) * rows + r + side))
    return lax.ppermute(value, ("layer", "row"), pairs)


def body(propagator, col_blocks, sources, incoming):
    ticks, _, shots, _ = sources.shape
    layers = lax.axis_size("layer")
    rows = lax.axis_size("row")
    cols = col_blocks[0].reshape(-1)
    cut = (shots // 16 + 1) // 2 * 16
    panels = [(0, cut), (cut, shots)]
    own = [incoming[0, a:b] for a, b in panels]
    weights = split_weights(jnp.transpose(propagator[0], (1, 0, 2)))
    history = []
    for tick in range(ticks):
        produced = []
        for i, (a, b) in enumerate(panels):
            gathered = lax.all_gather(own[i], "row", axis=0)
            done = apply_layer(cols, weights, gathered, sources[tick, 0, a:b])
            produced.append(done)
            if tick + 1 < ticks:
                own[i] = hop(done, layers, rows, 1, 0)
        history.append(jnp.concatenate(produced, axis=0))
    return jnp.stack(history)[:, None]


def solution(mesh):
    return jax.shard_map(
        body,
        mesh=mesh,
        in_specs=(
            P("layer", "row", None, None),
            P("layer", "row", None),
            P(None, "layer", None, "row"),
            P("layer", None, "row"),
        ),
        out_specs=P(None, "layer", None, "row"),
        check_vma=False,
    )
```

```python
import functools

import jax
import jax.numpy as jnp
from jax import lax
from jax.experimental import pallas as pl
from jax.experimental.pallas import tpu as pltpu
from jax.sharding import PartitionSpec as P

MIB = 1024 * 1024


def split_kernel(prop_ref, weights_ref, blocks, arrived):
    row_blocks, depth, twice = weights_ref.shape
    flight, slots, blk, _ = blocks.shape

    def fetch(r, slot):
        rows = pl.ds(pl.multiple_of(r * blk, blk), blk)
        return pltpu.make_async_copy(prop_ref.at[:, rows, :], blocks.at[slot], arrived.at[slot])

    for r in range(flight):
        fetch(r, r).start()

    def step(r, carry):
        slot = lax.rem(r, flight)
        fetch(r, slot).wait()
        for k in range(slots):
            block = blocks[slot, k].T
            high = block.astype(jnp.bfloat16)
            low = (block - high.astype(jnp.float32)).astype(jnp.bfloat16)
            weights_ref[r, k * blk:(k + 1) * blk, :blk] = high
            weights_ref[r, k * blk:(k + 1) * blk, blk:] = low

        @pl.when(r + flight < row_blocks)
        def _():
            fetch(r + flight, slot).start()

        return carry

    lax.fori_loop(0, row_blocks, step, 0)


def split_weights(prop):
    slots, rows, blk = prop.shape
    flight = min(8, rows // blk)
    return pl.pallas_call(
        split_kernel,
        in_specs=[pl.BlockSpec(memory_space=pl.ANY)],
        out_specs=pl.BlockSpec(memory_space=pltpu.VMEM),
        out_shape=jax.ShapeDtypeStruct((rows // blk, slots * blk, 2 * blk), jnp.bfloat16),
        scratch_shapes=[
            pltpu.VMEM((flight, slots, blk, blk), jnp.float32),
            pltpu.SemaphoreType.DMA((flight,)),
        ],
        compiler_params=pltpu.CompilerParams(vmem_limit_bytes=8 * MIB),
        cost_estimate=pl.CostEstimate(flops=0, bytes_accessed=prop.size * 4, transcendentals=0),
        name="split_weights",
    )(prop)


def tick_kernel(cols_ref, weights_ref, left_ref, own_ref, right_ref, source_ref, out_ref, window):
    width = own_ref.shape[1]
    row_blocks, depth, twice = weights_ref.shape
    blk = twice // 2
    slots = depth // blk
    window[:, :width] = left_ref[...]
    window[:, width:2 * width] = own_ref[...]
    window[:, 2 * width:] = right_ref[...]

    def step(r, carry):
        picked = []
        for k in range(slots):
            start = pl.multiple_of(cols_ref[r * slots + k] * blk, blk)
            picked.append(window[:, pl.ds(start, blk)])
        both = jnp.dot(jnp.concatenate(picked, axis=1), weights_ref[r], preferred_element_type=jnp.float32)
        here = pl.ds(pl.multiple_of(r * blk, blk), blk)
        total = both[:, :blk] + both[:, blk:] + source_ref[:, here].astype(jnp.float32)
        out_ref[:, here] = total.astype(out_ref.dtype)
        return carry

    lax.fori_loop(0, row_blocks, step, 0, unroll=4)


def apply_layer(cols, weights, left, own, right, source):
    shots, width = own.shape
    vmem = pl.BlockSpec(memory_space=pltpu.VMEM)
    return pl.pallas_call(
        tick_kernel,
        in_specs=[pl.BlockSpec(memory_space=pltpu.SMEM)] + [vmem] * 5,
        out_specs=vmem,
        out_shape=jax.ShapeDtypeStruct((shots, width), jnp.bfloat16),
        scratch_shapes=[pltpu.VMEM((shots, 3 * width), jnp.bfloat16)],
        compiler_params=pltpu.CompilerParams(vmem_limit_bytes=8 * MIB),
        cost_estimate=pl.CostEstimate(
            flops=2 * shots * weights.size, bytes_accessed=weights.size * 2, transcendentals=0
        ),
        name="apply_layer",
    )(cols, weights, left, own, right, source)


def hop(value, layers, rows, up, side):
    pairs = []
    for l in range(layers - up):
        for r in range(rows):
            if 0 <= r + side < rows:
                pairs.append((l * rows + r, (l + up) * rows + r + side))
    return lax.ppermute(value, ("layer", "row"), pairs)


def body(propagator, col_blocks, sources, incoming):
    _, row_count, slots, blk = propagator.shape
    ticks, _, shots, _ = sources.shape
    layers = lax.axis_size("layer")
    rows = lax.axis_size("row")
    block_count = row_count // blk
    cols = (col_blocks[0] - (lax.axis_index("row") - 1) * block_count).reshape(-1)
    cut = (shots // 16 + 1) // 2 * 16
    panels = [(0, cut), (cut, shots)]
    arriving = []
    for a, b in panels:
        own = incoming[0, a:b]
        arriving.append((hop(own, layers, rows, 0, 1), own, hop(own, layers, rows, 0, -1)))
    weights = split_weights(jnp.transpose(propagator[0], (1, 0, 2)))
    history = []
    for tick in range(ticks):
        produced = []
        for i, (a, b) in enumerate(panels):
            done = apply_layer(cols, weights, *arriving[i], sources[tick, 0, a:b])
            produced.append(done)
            if tick + 1 < ticks:
                arriving[i] = tuple(hop(done, layers, rows, 1, side) for side in (1, 0, -1))
        history.append(jnp.concatenate(produced, axis=0))
    return jnp.stack(history)[:, None]


def solution(mesh):
    return jax.shard_map(
        body,
        mesh=mesh,
        in_specs=(
            P("layer", "row", None, None),
            P("layer", "row", None),
            P(None, "layer", None, "row"),
            P("layer", None, "row"),
        ),
        out_specs=P(None, "layer", None, "row"),
        check_vma=False,
    )
```

```python
import functools

import jax
import jax.numpy as jnp
from jax import lax
from jax.experimental import pallas as pl
from jax.experimental.pallas import tpu as pltpu
from jax.sharding import PartitionSpec as P

MIB = 1024 * 1024


def convert_kernel(prop_ref, weights_ref, blocks, arrived):
    row_blocks = weights_ref.shape[0]
    flight, slots, blk, _ = blocks.shape

    def fetch(r, slot):
        rows = pl.ds(pl.multiple_of(r * blk, blk), blk)
        return pltpu.make_async_copy(prop_ref.at[:, rows, :], blocks.at[slot], arrived.at[slot])

    for r in range(flight):
        fetch(r, r).start()

    def step(r, carry):
        slot = lax.rem(r, flight)
        fetch(r, slot).wait()
        for k in range(slots):
            weights_ref[r, k * blk:(k + 1) * blk, :] = blocks[slot, k].astype(jnp.bfloat16).T

        @pl.when(r + flight < row_blocks)
        def _():
            fetch(r + flight, slot).start()

        return carry

    lax.fori_loop(0, row_blocks, step, 0)


def convert_weights(prop):
    slots, rows, blk = prop.shape
    flight = min(8, rows // blk)
    return pl.pallas_call(
        convert_kernel,
        in_specs=[pl.BlockSpec(memory_space=pltpu.HBM)],
        out_specs=pl.BlockSpec(memory_space=pltpu.VMEM),
        out_shape=jax.ShapeDtypeStruct((rows // blk, slots * blk, blk), jnp.bfloat16),
        scratch_shapes=[
            pltpu.VMEM((flight, slots, blk, blk), jnp.float32),
            pltpu.SemaphoreType.DMA((flight,)),
        ],
        compiler_params=pltpu.CompilerParams(vmem_limit_bytes=48 * MIB),
        cost_estimate=pl.CostEstimate(flops=0, bytes_accessed=prop.size * 4, transcendentals=0),
        name="convert_weights",
    )(prop)


def tick_kernel(cols_ref, weights_ref, left_ref, own_ref, right_ref, source_ref, out_ref, window):
    width = own_ref.shape[1]
    row_blocks, depth, blk = weights_ref.shape
    slots = depth // blk
    window[:, :width] = left_ref[...]
    window[:, width:2 * width] = own_ref[...]
    window[:, 2 * width:] = right_ref[...]

    def step(r, carry):
        picked = []
        for k in range(slots):
            start = pl.multiple_of(cols_ref[r * slots + k] * blk, blk)
            picked.append(window[:, pl.ds(start, blk)])
        mixed = jnp.dot(jnp.concatenate(picked, axis=1), weights_ref[r], preferred_element_type=jnp.float32)
        here = pl.ds(pl.multiple_of(r * blk, blk), blk)
        out_ref[:, here] = (mixed + source_ref[:, here].astype(jnp.float32)).astype(out_ref.dtype)
        return carry

    lax.fori_loop(0, row_blocks, step, 0, unroll=8)


def apply_layer(cols, weights, left, own, right, source):
    shots, width = own.shape
    vmem = pl.BlockSpec(memory_space=pltpu.VMEM)
    return pl.pallas_call(
        tick_kernel,
        in_specs=[pl.BlockSpec(memory_space=pltpu.SMEM)] + [vmem] * 5,
        out_specs=vmem,
        out_shape=jax.ShapeDtypeStruct((shots, width), jnp.bfloat16),
        scratch_shapes=[pltpu.VMEM((shots, 3 * width), jnp.bfloat16)],
        compiler_params=pltpu.CompilerParams(vmem_limit_bytes=8 * MIB),
        cost_estimate=pl.CostEstimate(
            flops=2 * shots * weights.size, bytes_accessed=weights.size * 2, transcendentals=0
        ),
        name="apply_layer",
    )(cols, weights, left, own, right, source)


def hop(value, layers, rows, up, side):
    pairs = []
    for l in range(layers - up):
        for r in range(rows):
            if 0 <= r + side < rows:
                pairs.append((l * rows + r, (l + up) * rows + r + side))
    return lax.ppermute(value, ("layer", "row"), pairs)


def body(propagator, col_blocks, sources, incoming):
    _, row_count, slots, blk = propagator.shape
    ticks, _, shots, _ = sources.shape
    layers = lax.axis_size("layer")
    rows = lax.axis_size("row")
    block_count = row_count // blk
    cols = (col_blocks[0] - (lax.axis_index("row") - 1) * block_count).reshape(-1)
    cut = (shots // 16 + 1) // 2 * 16
    panels = [(0, cut), (cut, shots)]
    arriving = []
    for a, b in panels:
        own = incoming[0, a:b]
        arriving.append((hop(own, layers, rows, 0, 1), own, hop(own, layers, rows, 0, -1)))
    weights = convert_weights(jnp.transpose(propagator[0], (1, 0, 2)))
    history = []
    for tick in range(ticks):
        produced = []
        for i, (a, b) in enumerate(panels):
            done = apply_layer(cols, weights, *arriving[i], sources[tick, 0, a:b])
            produced.append(done)
            if tick + 1 < ticks:
                arriving[i] = tuple(hop(done, layers, rows, 1, side) for side in (1, 0, -1))
        history.append(jnp.concatenate(produced, axis=0))
    return jnp.stack(history)[:, None]


def solution(mesh):
    return jax.shard_map(
        body,
        mesh=mesh,
        in_specs=(
            P("layer", "row", None, None),
            P("layer", "row", None),
            P(None, "layer", None, "row"),
            P("layer", None, "row"),
        ),
        out_specs=P(None, "layer", None, "row"),
        check_vma=False,
    )
```

```python
import functools

import jax
import jax.numpy as jnp
from jax import lax
from jax.experimental import pallas as pl
from jax.experimental.pallas import tpu as pltpu
from jax.sharding import PartitionSpec as P

MIB = 1024 * 1024


def convert_kernel(prop_ref, weights_ref, blocks, arrived):
    row_blocks = weights_ref.shape[0]
    flight, slots, blk, _ = blocks.shape

    def fetch(r, slot):
        rows = pl.ds(pl.multiple_of(r * blk, blk), blk)
        return pltpu.make_async_copy(prop_ref.at[:, rows, :], blocks.at[slot], arrived.at[slot])

    for r in range(flight):
        fetch(r, r).start()

    def step(r, carry):
        slot = lax.rem(r, flight)
        fetch(r, slot).wait()
        for k in range(slots):
            weights_ref[r, k * blk:(k + 1) * blk, :] = blocks[slot, k].astype(jnp.bfloat16).T

        @pl.when(r + flight < row_blocks)
        def _():
            fetch(r + flight, slot).start()

        return carry

    lax.fori_loop(0, row_blocks, step, 0)


def convert_weights(prop):
    slots, rows, blk = prop.shape
    flight = min(8, rows // blk)
    return pl.pallas_call(
        convert_kernel,
        in_specs=[pl.BlockSpec(memory_space=pltpu.HBM)],
        out_specs=pl.BlockSpec(memory_space=pltpu.VMEM),
        out_shape=jax.ShapeDtypeStruct((rows // blk, slots * blk, blk), jnp.bfloat16),
        scratch_shapes=[
            pltpu.VMEM((flight, slots, blk, blk), jnp.float32),
            pltpu.SemaphoreType.DMA((flight,)),
        ],
        compiler_params=pltpu.CompilerParams(vmem_limit_bytes=48 * MIB),
        cost_estimate=pl.CostEstimate(flops=0, bytes_accessed=prop.size * 4, transcendentals=0),
        name="convert_weights",
    )(prop)


def tick_kernel(cols_ref, weights_ref, far_ref, near_ref, own_ref, source_ref, before_ref, out_ref, window):
    del before_ref
    width = own_ref.shape[1]
    row_blocks, depth, blk = weights_ref.shape
    slots = depth // blk
    window[:, :width] = near_ref[...]
    window[:, width:2 * width] = own_ref[...]
    window[:, 2 * width:] = far_ref[...]

    def step(r, carry):
        picked = []
        for k in range(slots):
            start = pl.multiple_of(cols_ref[r * slots + k] * blk, blk)
            picked.append(window[:, pl.ds(start, blk)])
        mixed = jnp.dot(jnp.concatenate(picked, axis=1), weights_ref[r], preferred_element_type=jnp.float32)
        here = pl.ds(pl.multiple_of(r * blk, blk), blk)
        out_ref[:, here] = (mixed + source_ref[:, here].astype(jnp.float32)).astype(out_ref.dtype)
        return carry

    lax.fori_loop(0, row_blocks, step, 0, unroll=8)


def apply_layer(cols, weights, far, near, own, source, before):
    shots, width = own.shape
    vmem = pl.BlockSpec(memory_space=pltpu.VMEM)
    return pl.pallas_call(
        tick_kernel,
        in_specs=[pl.BlockSpec(memory_space=pltpu.SMEM)] + [vmem] * 5 + [pl.BlockSpec(memory_space=pl.ANY)],
        out_specs=vmem,
        out_shape=jax.ShapeDtypeStruct((shots, width), jnp.bfloat16),
        scratch_shapes=[pltpu.VMEM((shots, 3 * width), jnp.bfloat16)],
        compiler_params=pltpu.CompilerParams(vmem_limit_bytes=8 * MIB),
        cost_estimate=pl.CostEstimate(
            flops=2 * shots * weights.size, bytes_accessed=weights.size * 2, transcendentals=0
        ),
        name="apply_layer",
    )(cols, weights, far, near, own, source, before)


def partner(r, rows, far):
    other = (r + 1 if r % 2 else r - 1) if far else r ^ 1
    return other if 0 <= other < rows else None


def send(value, layers, up, targets):
    rows = len(targets)
    pairs = []
    for l in range(layers - up):
        for r, target in enumerate(targets):
            if target is not None:
                pairs.append((l * rows + r, (l + up) * rows + target))
    return lax.ppermute(value, ("layer", "row"), pairs)


def body(propagator, col_blocks, sources, incoming):
    _, row_count, slots, blk = propagator.shape
    ticks, _, shots, _ = sources.shape
    layers = lax.axis_size("layer")
    rows = lax.axis_size("row")
    near = [partner(r, rows, False) for r in range(rows)]
    far = [partner(r, rows, True) for r in range(rows)]
    block_count = row_count // blk
    place = lax.axis_index("row")
    side = lax.div(col_blocks[0], block_count) - place
    third = 1 + side * (2 * lax.rem(place, 2) - 1)
    cols = (third * block_count + lax.rem(col_blocks[0], block_count)).reshape(-1)
    cut = (shots // 16 + 1) // 2 * 16
    panels = [(0, cut), (cut, shots)]
    arriving = []
    for a, b in panels:
        own = incoming[0, a:b]
        distant = send(own, layers, 0, far)
        arriving.append((distant, send(own, layers, 0, near), own))
    weights = convert_weights(jnp.transpose(propagator[0], (1, 0, 2)))
    before = weights
    history = []
    for tick in range(ticks):
        produced = []
        for i, (a, b) in enumerate(panels):
            done = apply_layer(cols, weights, *arriving[i], sources[tick, 0, a:b], before)
            before = done
            produced.append(done)
            if tick + 1 < ticks:
                distant = send(done, layers, 1, far)
                beside = send(done, layers, 1, near)
                arriving[i] = (distant, beside, send(done, layers, 1, range(rows)))
        history.append(jnp.concatenate(produced, axis=0))
    return jnp.stack(history)[:, None]


def solution(mesh):
    return jax.shard_map(
        body,
        mesh=mesh,
        in_specs=(
            P("layer", "row", None, None),
            P("layer", "row", None),
            P(None, "layer", None, "row"),
            P("layer", None, "row"),
        ),
        out_specs=P(None, "layer", None, "row"),
        check_vma=False,
    )
```

```python
import functools

import jax
import jax.numpy as jnp
from jax import lax
from jax.experimental import pallas as pl
from jax.experimental.pallas import tpu as pltpu
from jax.sharding import PartitionSpec as P

MIB = 1024 * 1024


def convert_kernel(prop_ref, weights_ref, blocks, arrived):
    row_blocks = weights_ref.shape[0]
    flight, slots, blk, _ = blocks.shape

    def fetch(r, slot):
        rows = pl.ds(pl.multiple_of(r * blk, blk), blk)
        return pltpu.make_async_copy(prop_ref.at[:, rows, :], blocks.at[slot], arrived.at[slot])

    for r in range(flight):
        fetch(r, r).start()

    def step(r, carry):
        slot = lax.rem(r, flight)
        fetch(r, slot).wait()
        for k in range(slots):
            weights_ref[r, k * blk:(k + 1) * blk, :] = blocks[slot, k].astype(jnp.bfloat16).T

        @pl.when(r + flight < row_blocks)
        def _():
            fetch(r + flight, slot).start()

        return carry

    lax.fori_loop(0, row_blocks, step, 0)


def convert_weights(prop):
    slots, rows, blk = prop.shape
    flight = min(8, rows // blk)
    return pl.pallas_call(
        convert_kernel,
        in_specs=[pl.BlockSpec(memory_space=pltpu.HBM)],
        out_specs=pl.BlockSpec(memory_space=pltpu.VMEM),
        out_shape=jax.ShapeDtypeStruct((rows // blk, slots * blk, blk), jnp.bfloat16),
        scratch_shapes=[
            pltpu.VMEM((flight, slots, blk, blk), jnp.float32),
            pltpu.SemaphoreType.DMA((flight,)),
        ],
        compiler_params=pltpu.CompilerParams(vmem_limit_bytes=44 * MIB),
        cost_estimate=pl.CostEstimate(flops=0, bytes_accessed=prop.size * 4, transcendentals=0),
        name="convert_weights",
    )(prop)


def tick_kernel(tick, first, cols_ref, weights_ref, far_ref, near_ref, own_ref, source_ref, before_ref, out_ref, window):
    del before_ref
    shots, width = own_ref.shape
    row_blocks, depth, blk = weights_ref.shape
    slots = depth // blk
    window[:, :width] = near_ref[...]
    window[:, width:2 * width] = own_ref[...]
    window[:, 2 * width:] = far_ref[...]

    def step(r, carry):
        picked = []
        for k in range(slots):
            start = pl.multiple_of(cols_ref[r * slots + k] * blk, blk)
            picked.append(window[:, pl.ds(start, blk)])
        mixed = jnp.dot(jnp.concatenate(picked, axis=1), weights_ref[r], preferred_element_type=jnp.float32)
        here = pl.ds(pl.multiple_of(r * blk, blk), blk)
        out_ref[:, here] = (mixed + source_ref[tick, 0, first:first + shots, here].astype(jnp.float32)).astype(out_ref.dtype)
        return carry

    lax.fori_loop(0, row_blocks, step, 0, unroll=8)


def apply_layer(tick, first, cols, weights, far, near, own, sources, before):
    shots, width = own.shape
    vmem = pl.BlockSpec(memory_space=pltpu.VMEM)
    return pl.pallas_call(
        functools.partial(tick_kernel, tick, first),
        in_specs=[pl.BlockSpec(memory_space=pltpu.SMEM)] + [vmem] * 5 + [pl.BlockSpec(memory_space=pl.ANY)],
        out_specs=vmem,
        out_shape=jax.ShapeDtypeStruct((shots, width), jnp.bfloat16),
        scratch_shapes=[pltpu.VMEM((shots, 3 * width), jnp.bfloat16)],
        compiler_params=pltpu.CompilerParams(vmem_limit_bytes=8 * MIB),
        cost_estimate=pl.CostEstimate(
            flops=2 * shots * weights.size, bytes_accessed=weights.size * 2, transcendentals=0
        ),
        name="apply_layer",
    )(cols, weights, far, near, own, sources, before)


def partner(r, rows, far):
    other = (r + 1 if r % 2 else r - 1) if far else r ^ 1
    return other if 0 <= other < rows else None


def send(value, layers, up, targets):
    rows = len(targets)
    pairs = []
    for l in range(layers - up):
        for r, target in enumerate(targets):
            if target is not None:
                pairs.append((l * rows + r, (l + up) * rows + target))
    return lax.ppermute(value, ("layer", "row"), pairs)


def body(propagator, col_blocks, sources, incoming):
    _, row_count, slots, blk = propagator.shape
    ticks, _, shots, _ = sources.shape
    layers = lax.axis_size("layer")
    rows = lax.axis_size("row")
    near = [partner(r, rows, False) for r in range(rows)]
    far = [partner(r, rows, True) for r in range(rows)]
    block_count = row_count // blk
    place = lax.axis_index("row")
    side = lax.div(col_blocks[0], block_count) - place
    third = 1 + side * (2 * lax.rem(place, 2) - 1)
    cols = (third * block_count + lax.rem(col_blocks[0], block_count)).reshape(-1)
    cut = (shots // 16 + 1) // 2 * 16
    panels = [(0, cut), (cut, shots)]
    arriving = []
    for a, b in panels:
        own = incoming[0, a:b]
        distant = send(own, layers, 0, far)
        arriving.append((distant, send(own, layers, 0, near), own))
    weights = convert_weights(jnp.transpose(propagator[0], (1, 0, 2)))
    before = weights
    history = []
    for tick in range(ticks):
        produced = []
        for i in range(len(panels)):
            done = apply_layer(tick, panels[i][0], cols, weights, *arriving[i], sources, before)
            before = done
            produced.append(done)
            if tick + 1 < ticks:
                distant = send(done, layers, 1, far)
                beside = send(done, layers, 1, near)
                arriving[i] = (distant, beside, send(done, layers, 1, range(rows)))
        history.append(jnp.concatenate(produced, axis=0))
    return jnp.stack(history)[:, None]


def solution(mesh):
    return jax.shard_map(
        body,
        mesh=mesh,
        in_specs=(
            P("layer", "row", None, None),
            P("layer", "row", None),
            P(None, "layer", None, "row"),
            P("layer", None, "row"),
        ),
        out_specs=P(None, "layer", None, "row"),
        check_vma=False,
    )
```

```python
import functools

import jax
import jax.numpy as jnp
from jax import lax
from jax.experimental import pallas as pl
from jax.experimental.pallas import tpu as pltpu
from jax.sharding import PartitionSpec as P

MIB = 1024 * 1024


def convert_kernel(prop_ref, weights_ref, blocks, arrived):
    row_blocks = weights_ref.shape[0]
    flight, slots, blk, _ = blocks.shape

    def fetch(r, slot):
        rows = pl.ds(pl.multiple_of(r * blk, blk), blk)
        return pltpu.make_async_copy(prop_ref.at[:, rows, :], blocks.at[slot], arrived.at[slot])

    for r in range(flight):
        fetch(r, r).start()

    def step(r, carry):
        slot = lax.rem(r, flight)
        fetch(r, slot).wait()
        for k in range(slots):
            weights_ref[r, k * blk:(k + 1) * blk, :] = blocks[slot, k].astype(jnp.bfloat16).T

        @pl.when(r + flight < row_blocks)
        def _():
            fetch(r + flight, slot).start()

        return carry

    lax.fori_loop(0, row_blocks, step, 0)


def convert_weights(prop):
    slots, rows, blk = prop.shape
    flight = min(8, rows // blk)
    return pl.pallas_call(
        convert_kernel,
        in_specs=[pl.BlockSpec(memory_space=pltpu.HBM)],
        out_specs=pl.BlockSpec(memory_space=pltpu.VMEM),
        out_shape=jax.ShapeDtypeStruct((rows // blk, slots * blk, blk), jnp.bfloat16),
        scratch_shapes=[
            pltpu.VMEM((flight, slots, blk, blk), jnp.float32),
            pltpu.SemaphoreType.DMA((flight,)),
        ],
        compiler_params=pltpu.CompilerParams(vmem_limit_bytes=44 * MIB),
        cost_estimate=pl.CostEstimate(flops=0, bytes_accessed=prop.size * 4, transcendentals=0),
        name="convert_weights",
    )(prop)


def tick_kernel(tick, first, cols_ref, weights_ref, near_ref, far_ref, own_ref, source_ref, before_ref, out_ref, window):
    del before_ref
    shots, width = own_ref.shape
    row_blocks, depth, blk = weights_ref.shape
    slots = depth // blk
    window[:, :width] = near_ref[...]
    window[:, width:2 * width] = own_ref[...]
    window[:, 2 * width:] = far_ref[...]

    def step(r, carry):
        picked = []
        for k in range(slots):
            start = pl.multiple_of(cols_ref[r * slots + k] * blk, blk)
            picked.append(window[:, pl.ds(start, blk)])
        mixed = jnp.dot(jnp.concatenate(picked, axis=1), weights_ref[r], preferred_element_type=jnp.float32)
        here = pl.ds(pl.multiple_of(r * blk, blk), blk)
        out_ref[:, here] = (mixed + source_ref[tick, 0, first:first + shots, here].astype(jnp.float32)).astype(out_ref.dtype)
        return carry

    lax.fori_loop(0, row_blocks, step, 0, unroll=min(16, row_blocks))


def apply_layer(tick, first, cols, weights, near, far, own, sources, before):
    shots, width = own.shape
    vmem = pl.BlockSpec(memory_space=pltpu.VMEM)
    return pl.pallas_call(
        functools.partial(tick_kernel, tick, first),
        in_specs=[pl.BlockSpec(memory_space=pltpu.SMEM)] + [vmem] * 5 + [pl.BlockSpec(memory_space=pl.ANY)],
        out_specs=vmem,
        out_shape=jax.ShapeDtypeStruct((shots, width), jnp.bfloat16),
        scratch_shapes=[pltpu.VMEM((shots, 3 * width), jnp.bfloat16)],
        compiler_params=pltpu.CompilerParams(vmem_limit_bytes=8 * MIB),
        cost_estimate=pl.CostEstimate(
            flops=2 * shots * weights.size, bytes_accessed=weights.size * 2, transcendentals=0
        ),
        name="apply_layer",
    )(cols, weights, near, far, own, sources, before)


def partner(r, rows, far):
    other = (r + 1 if r % 2 else r - 1) if far else r ^ 1
    return other if 0 <= other < rows else None


def send(value, layers, up, targets):
    rows = len(targets)
    pairs = []
    for l in range(layers - up):
        for r, target in enumerate(targets):
            if target is not None:
                pairs.append((l * rows + r, (l + up) * rows + target))
    return lax.ppermute(value, ("layer", "row"), pairs)


def body(propagator, col_blocks, sources, incoming):
    _, row_count, slots, blk = propagator.shape
    ticks, _, shots, _ = sources.shape
    layers = lax.axis_size("layer")
    rows = lax.axis_size("row")
    near = [partner(r, rows, False) for r in range(rows)]
    far = [partner(r, rows, True) for r in range(rows)]
    block_count = row_count // blk
    place = lax.axis_index("row")
    side = lax.div(col_blocks[0], block_count) - place
    third = 1 + side * (2 * lax.rem(place, 2) - 1)
    cols = (third * block_count + lax.rem(col_blocks[0], block_count)).reshape(-1)
    cut = (shots // 16 + 1) // 2 * 16
    panels = [(0, cut), (cut, shots)]
    arriving = []
    for a, b in panels:
        own = incoming[0, a:b]
        beside = send(own, layers, 0, near)
        arriving.append((beside, send(own, layers, 0, far), own))
    weights = convert_weights(jnp.transpose(propagator[0], (1, 0, 2)))
    before = weights
    history = []
    for tick in range(ticks):
        produced = []
        for i in range(len(panels)):
            done = apply_layer(tick, panels[i][0], cols, weights, *arriving[i], sources, before)
            before = done
            produced.append(done)
            if tick + 1 < ticks:
                beside = send(done, layers, 1, near)
                distant = send(done, layers, 1, far)
                arriving[i] = (beside, distant, send(done, layers, 1, range(rows)))
        history.append(jnp.concatenate(produced, axis=0))
    return jnp.stack(history)[:, None]


def solution(mesh):
    return jax.shard_map(
        body,
        mesh=mesh,
        in_specs=(
            P("layer", "row", None, None),
            P("layer", "row", None),
            P(None, "layer", None, "row"),
            P("layer", None, "row"),
        ),
        out_specs=P(None, "layer", None, "row"),
        check_vma=False,
    )
```

```python
import functools

import jax
import jax.numpy as jnp
from jax import lax
from jax.experimental import pallas as pl
from jax.experimental.pallas import tpu as pltpu
from jax.sharding import PartitionSpec as P

MIB = 1024 * 1024


def convert_kernel(prop_ref, weights_ref, blocks, arrived):
    row_blocks = weights_ref.shape[0]
    flight, slots, blk, _ = blocks.shape

    def fetch(r, slot):
        rows = pl.ds(pl.multiple_of(r * blk, blk), blk)
        return pltpu.make_async_copy(prop_ref.at[:, rows, :], blocks.at[slot], arrived.at[slot])

    for r in range(flight):
        fetch(r, r).start()

    def step(r, carry):
        slot = lax.rem(r, flight)
        fetch(r, slot).wait()
        for k in range(slots):
            weights_ref[r, k * blk:(k + 1) * blk, :] = blocks[slot, k].astype(jnp.bfloat16).T

        @pl.when(r + flight < row_blocks)
        def _():
            fetch(r + flight, slot).start()

        return carry

    lax.fori_loop(0, row_blocks, step, 0)


def convert_weights(prop):
    slots, rows, blk = prop.shape
    flight = min(8, rows // blk)
    return pl.pallas_call(
        convert_kernel,
        in_specs=[pl.BlockSpec(memory_space=pltpu.HBM)],
        out_specs=pl.BlockSpec(memory_space=pltpu.VMEM),
        out_shape=jax.ShapeDtypeStruct((rows // blk, slots * blk, blk), jnp.bfloat16),
        scratch_shapes=[
            pltpu.VMEM((flight, slots, blk, blk), jnp.float32),
            pltpu.SemaphoreType.DMA((flight,)),
        ],
        compiler_params=pltpu.CompilerParams(vmem_limit_bytes=44 * MIB),
        cost_estimate=pl.CostEstimate(flops=0, bytes_accessed=prop.size * 4, transcendentals=0),
        name="convert_weights",
    )(prop)


def tick_kernel(tick, first, cols_ref, weights_ref, near_ref, own_ref, far_ref, source_ref, before_ref, out_ref, window):
    del before_ref
    shots, width = own_ref.shape
    row_blocks, depth, blk = weights_ref.shape
    slots = depth // blk
    window[:, :width] = near_ref[...]
    window[:, width:2 * width] = own_ref[...]
    window[:, 2 * width:] = far_ref[...]

    def step(r, carry):
        picked = []
        for k in range(slots):
            start = pl.multiple_of(cols_ref[r * slots + k] * blk, blk)
            picked.append(window[:, pl.ds(start, blk)])
        mixed = jnp.dot(jnp.concatenate(picked, axis=1), weights_ref[r], preferred_element_type=jnp.float32)
        here = pl.ds(pl.multiple_of(r * blk, blk), blk)
        out_ref[:, here] = (mixed + source_ref[tick, 0, first:first + shots, here].astype(jnp.float32)).astype(out_ref.dtype)
        return carry

    lax.fori_loop(0, row_blocks, step, 0, unroll=min(16, row_blocks))


def apply_layer(tick, first, cols, weights, near, own, far, sources, before):
    shots, width = own.shape
    vmem = pl.BlockSpec(memory_space=pltpu.VMEM)
    return pl.pallas_call(
        functools.partial(tick_kernel, tick, first),
        in_specs=[pl.BlockSpec(memory_space=pltpu.SMEM)] + [vmem] * 5 + [pl.BlockSpec(memory_space=pl.ANY)],
        out_specs=vmem,
        out_shape=jax.ShapeDtypeStruct((shots, width), jnp.bfloat16),
        scratch_shapes=[pltpu.VMEM((shots, 3 * width), jnp.bfloat16)],
        compiler_params=pltpu.CompilerParams(vmem_limit_bytes=8 * MIB),
        cost_estimate=pl.CostEstimate(
            flops=2 * shots * weights.size, bytes_accessed=weights.size * 2, transcendentals=0
        ),
        name="apply_layer",
    )(cols, weights, near, own, far, sources, before)


def partner(r, rows, far):
    other = (r + 1 if r % 2 else r - 1) if far else r ^ 1
    return other if 0 <= other < rows else None


def send(value, layers, up, targets):
    rows = len(targets)
    pairs = []
    for l in range(layers - up):
        for r, target in enumerate(targets):
            if target is not None:
                pairs.append((l * rows + r, (l + up) * rows + target))
    return lax.ppermute(value, ("layer", "row"), pairs)


def body(propagator, col_blocks, sources, incoming):
    _, row_count, slots, blk = propagator.shape
    ticks, _, shots, _ = sources.shape
    layers = lax.axis_size("layer")
    rows = lax.axis_size("row")
    near = [partner(r, rows, False) for r in range(rows)]
    far = [partner(r, rows, True) for r in range(rows)]
    block_count = row_count // blk
    place = lax.axis_index("row")
    side = lax.div(col_blocks[0], block_count) - place
    third = 1 + side * (2 * lax.rem(place, 2) - 1)
    cols = (third * block_count + lax.rem(col_blocks[0], block_count)).reshape(-1)
    cut = (shots // 16 + 1) // 2 * 16
    panels = [(0, cut), (cut, shots)]
    arriving = []
    for a, b in panels:
        own = incoming[0, a:b]
        beside = send(own, layers, 0, near)
        arriving.append((beside, own, send(own, layers, 0, far)))
    weights = convert_weights(jnp.transpose(propagator[0], (1, 0, 2)))
    before = weights
    history = []
    for tick in range(ticks):
        produced = []
        for i in range(len(panels)):
            done = apply_layer(tick, panels[i][0], cols, weights, *arriving[i], sources, before)
            before = done
            produced.append(done)
            if tick + 1 < ticks:
                beside = send(done, layers, 1, near)
                same = send(done, layers, 1, range(rows))
                distant = send(done, layers, 1, far)
                arriving[i] = (beside, same, distant)
        history.append(jnp.concatenate(produced, axis=0))
    return jnp.stack(history)[:, None]


def solution(mesh):
    return jax.shard_map(
        body,
        mesh=mesh,
        in_specs=(
            P("layer", "row", None, None),
            P("layer", "row", None),
            P(None, "layer", None, "row"),
            P("layer", None, "row"),
        ),
        out_specs=P(None, "layer", None, "row"),
        check_vma=False,
    )
```

```python
import functools

import jax
import jax.numpy as jnp
from jax import lax
from jax.experimental import pallas as pl
from jax.experimental.pallas import tpu as pltpu
from jax.sharding import PartitionSpec as P

MIB = 1024 * 1024


def convert_kernel(prop_ref, weights_ref, blocks, arrived):
    row_blocks = weights_ref.shape[0]
    flight, slots, blk, _ = blocks.shape

    def fetch(r, slot):
        rows = pl.ds(pl.multiple_of(r * blk, blk), blk)
        return pltpu.make_async_copy(prop_ref.at[:, rows, :], blocks.at[slot], arrived.at[slot])

    for r in range(flight):
        fetch(r, r).start()

    def step(r, carry):
        slot = lax.rem(r, flight)
        fetch(r, slot).wait()
        for k in range(slots):
            weights_ref[r, k * blk:(k + 1) * blk, :] = blocks[slot, k].astype(jnp.bfloat16).T

        @pl.when(r + flight < row_blocks)
        def _():
            fetch(r + flight, slot).start()

        return carry

    lax.fori_loop(0, row_blocks, step, 0)


def convert_weights(prop):
    slots, rows, blk = prop.shape
    flight = min(8, rows // blk)
    return pl.pallas_call(
        convert_kernel,
        in_specs=[pl.BlockSpec(memory_space=pltpu.HBM)],
        out_specs=pl.BlockSpec(memory_space=pltpu.VMEM),
        out_shape=jax.ShapeDtypeStruct((rows // blk, slots * blk, blk), jnp.bfloat16),
        scratch_shapes=[
            pltpu.VMEM((flight, slots, blk, blk), jnp.float32),
            pltpu.SemaphoreType.DMA((flight,)),
        ],
        compiler_params=pltpu.CompilerParams(vmem_limit_bytes=44 * MIB),
        cost_estimate=pl.CostEstimate(flops=0, bytes_accessed=prop.size * 4, transcendentals=0),
        name="convert_weights",
    )(prop)


def tick_kernel(tick, first, places, cols_ref, weights_ref, *refs):
    thirds, (source_ref, _, out_ref, window) = refs[:len(places)], refs[len(places):]
    shots, width = out_ref.shape
    row_blocks, depth, blk = weights_ref.shape
    slots = depth // blk
    for place, third_ref in zip(places, thirds):
        window[:, place * width:(place + 1) * width] = third_ref[...]

    def step(r, carry):
        picked = []
        for k in range(slots):
            start = pl.multiple_of(cols_ref[r * slots + k] * blk, blk)
            picked.append(window[:, pl.ds(start, blk)])
        mixed = jnp.dot(jnp.concatenate(picked, axis=1), weights_ref[r], preferred_element_type=jnp.float32)
        here = pl.ds(pl.multiple_of(r * blk, blk), blk)
        out_ref[:, here] = (mixed + source_ref[tick, 0, first:first + shots, here].astype(jnp.float32)).astype(out_ref.dtype)
        return carry

    lax.fori_loop(0, row_blocks, step, 0, unroll=True)


def apply_layer(tick, first, places, cols, weights, thirds, sources, before):
    shots, width = thirds[0].shape
    vmem = pl.BlockSpec(memory_space=pltpu.VMEM)
    return pl.pallas_call(
        functools.partial(tick_kernel, tick, first, places),
        in_specs=[pl.BlockSpec(memory_space=pltpu.SMEM)] + [vmem] * 5 + [pl.BlockSpec(memory_space=pl.ANY)],
        out_specs=vmem,
        out_shape=jax.ShapeDtypeStruct((shots, width), jnp.bfloat16),
        scratch_shapes=[pltpu.VMEM((shots, 3 * width), jnp.bfloat16)],
        compiler_params=pltpu.CompilerParams(vmem_limit_bytes=8 * MIB),
        cost_estimate=pl.CostEstimate(
            flops=2 * shots * weights.size, bytes_accessed=weights.size * 2, transcendentals=0
        ),
        name="apply_layer",
    )(cols, weights, *thirds, sources, before)


def partner(r, rows, far):
    other = (r + 1 if r % 2 else r - 1) if far else r ^ 1
    return other if 0 <= other < rows else None


def send(value, layers, up, targets):
    rows = len(targets)
    pairs = []
    for l in range(layers - up):
        for r, target in enumerate(targets):
            if target is not None:
                pairs.append((l * rows + r, (l + up) * rows + target))
    return lax.ppermute(value, ("layer", "row"), pairs)


def body(propagator, col_blocks, sources, incoming):
    _, row_count, slots, blk = propagator.shape
    ticks, _, shots, _ = sources.shape
    layers = lax.axis_size("layer")
    rows = lax.axis_size("row")
    near = [partner(r, rows, False) for r in range(rows)]
    far = [partner(r, rows, True) for r in range(rows)]
    block_count = row_count // blk
    place = lax.axis_index("row")
    side = lax.div(col_blocks[0], block_count) - place
    third = 1 + side * (2 * lax.rem(place, 2) - 1)
    cols = (third * block_count + lax.rem(col_blocks[0], block_count)).reshape(-1)
    cut = (shots // 16 + 1) // 2 * 16
    panels = [(0, cut), (cut, shots)]
    orders = [(0, 2, 1), (0, 1, 2)]
    arriving = []
    for a, b in panels:
        own = incoming[0, a:b]
        beside = send(own, layers, 0, near)
        arriving.append((beside, own, send(own, layers, 0, far)))
    weights = convert_weights(jnp.transpose(propagator[0], (1, 0, 2)))
    before = weights
    history = []
    for tick in range(ticks):
        produced = []
        for i in range(len(panels)):
            thirds = [arriving[i][place] for place in orders[i]]
            done = apply_layer(tick, panels[i][0], orders[i], cols, weights, thirds, sources, before)
            before = done
            produced.append(done)
            if tick + 1 < ticks:
                beside = send(done, layers, 1, near)
                same = send(done, layers, 1, range(rows))
                distant = send(done, layers, 1, far)
                arriving[i] = (beside, same, distant)
        history.append(jnp.concatenate(produced, axis=0))
    return jnp.stack(history)[:, None]


def solution(mesh):
    return jax.shard_map(
        body,
        mesh=mesh,
        in_specs=(
            P("layer", "row", None, None),
            P("layer", "row", None),
            P(None, "layer", None, "row"),
            P("layer", None, "row"),
        ),
        out_specs=P(None, "layer", None, "row"),
        check_vma=False,
    )
```

```python
import functools

import jax
import jax.numpy as jnp
from jax import lax
from jax.experimental import pallas as pl
from jax.experimental.pallas import tpu as pltpu
from jax.sharding import PartitionSpec as P

MIB = 1024 * 1024


def convert_kernel(prop_ref, weights_ref, blocks, arrived):
    row_blocks, _, blk = weights_ref.shape
    flight, slots, rows, _ = blocks.shape
    group = rows // blk
    steps = row_blocks // group

    def fetch(i, slot):
        here = pl.ds(pl.multiple_of(i * rows, rows), rows)
        return pltpu.make_async_copy(prop_ref.at[:, here, :], blocks.at[slot], arrived.at[slot])

    for i in range(flight):
        fetch(i, i).start()

    def step(i, carry):
        slot = lax.rem(i, flight)
        fetch(i, slot).wait()
        for g in range(group):
            for k in range(slots):
                block = blocks[slot, k, g * blk:(g + 1) * blk, :].astype(jnp.bfloat16)
                weights_ref[i * group + g, k * blk:(k + 1) * blk, :] = block.T

        @pl.when(i + flight < steps)
        def _():
            fetch(i + flight, slot).start()

        return carry

    lax.fori_loop(0, steps, step, 0)


def convert_weights(prop):
    slots, rows, blk = prop.shape
    group = 1 if rows // blk % 2 else 2
    flight = min(6, rows // blk // group)
    return pl.pallas_call(
        convert_kernel,
        in_specs=[pl.BlockSpec(memory_space=pltpu.HBM)],
        out_specs=pl.BlockSpec(memory_space=pltpu.VMEM),
        out_shape=jax.ShapeDtypeStruct((rows // blk, slots * blk, blk), jnp.bfloat16),
        scratch_shapes=[
            pltpu.VMEM((flight, slots, group * blk, blk), jnp.float32),
            pltpu.SemaphoreType.DMA((flight,)),
        ],
        compiler_params=pltpu.CompilerParams(vmem_limit_bytes=44 * MIB),
        cost_estimate=pl.CostEstimate(flops=0, bytes_accessed=prop.size * 4, transcendentals=0),
        name="convert_weights",
    )(prop)


def tick_kernel(tick, first, cols_ref, weights_ref, *refs):
    thirds, (source_ref, _, out_ref, window) = refs[:3], refs[3:]
    shots, width = out_ref.shape
    row_blocks, depth, blk = weights_ref.shape
    slots = depth // blk
    for place, third_ref in enumerate(thirds):
        window[:, place * width:(place + 1) * width] = third_ref[...]

    def step(r, carry):
        picked = []
        for k in range(slots):
            start = pl.multiple_of(cols_ref[k, r] * blk, blk)
            picked.append(window[:, pl.ds(start, blk)])
        mixed = jnp.dot(jnp.concatenate(picked, axis=1), weights_ref[r], preferred_element_type=jnp.float32)
        here = pl.ds(pl.multiple_of(r * blk, blk), blk)
        out_ref[:, here] = (mixed + source_ref[tick, 0, first:first + shots, here].astype(jnp.float32)).astype(out_ref.dtype)
        return carry

    lax.fori_loop(0, row_blocks, step, 0, unroll=True)


def apply_layer(tick, first, cols, weights, thirds, sources, before):
    shots, width = thirds[0].shape
    vmem = pl.BlockSpec(memory_space=pltpu.VMEM)
    return pl.pallas_call(
        functools.partial(tick_kernel, tick, first),
        in_specs=[pl.BlockSpec(memory_space=pltpu.SMEM)] + [vmem] * 5 + [pl.BlockSpec(memory_space=pl.ANY)],
        out_specs=vmem,
        out_shape=jax.ShapeDtypeStruct((shots, width), jnp.bfloat16),
        scratch_shapes=[pltpu.VMEM((shots, 3 * width), jnp.bfloat16)],
        compiler_params=pltpu.CompilerParams(vmem_limit_bytes=8 * MIB),
        cost_estimate=pl.CostEstimate(
            flops=2 * shots * weights.size, bytes_accessed=weights.size * 2, transcendentals=0
        ),
        name="apply_layer",
    )(cols, weights, *thirds, sources, before)


def partner(r, rows, far):
    other = (r + 1 if r % 2 else r - 1) if far else r ^ 1
    return other if 0 <= other < rows else None


def send(value, layers, up, targets):
    rows = len(targets)
    pairs = []
    for l in range(layers - up):
        for r, target in enumerate(targets):
            if target is not None:
                pairs.append((l * rows + r, (l + up) * rows + target))
    return lax.ppermute(value, ("layer", "row"), pairs)


def body(propagator, col_blocks, sources, incoming):
    _, row_count, slots, blk = propagator.shape
    ticks, _, shots, _ = sources.shape
    layers = lax.axis_size("layer")
    rows = lax.axis_size("row")
    near = [partner(r, rows, False) for r in range(rows)]
    far = [partner(r, rows, True) for r in range(rows)]
    block_count = row_count // blk
    place = lax.axis_index("row")
    absolute = jnp.transpose(col_blocks[0])
    side = lax.div(absolute, block_count) - place
    third = 1 + side * (2 * lax.rem(place, 2) - 1)
    cols = third * block_count + lax.rem(absolute, block_count)
    cut = (shots // 16 + 1) // 2 * 16
    panels = [(0, cut), (cut, shots)]
    arriving = []
    for a, b in panels:
        own = incoming[0, a:b]
        beside = send(own, layers, 0, near)
        arriving.append((beside, own, send(own, layers, 0, far)))
    weights = convert_weights(jnp.transpose(propagator[0], (1, 0, 2)))
    before = weights
    history = []
    for tick in range(ticks):
        produced = []
        for i in range(len(panels)):
            done = apply_layer(tick, panels[i][0], cols, weights, arriving[i], sources, before)
            before = done
            produced.append(done)
            if tick + 1 < ticks:
                beside = send(done, layers, 1, near)
                same = send(done, layers, 1, range(rows))
                distant = send(done, layers, 1, far)
                arriving[i] = (beside, same, distant)
        history.append(jnp.concatenate(produced, axis=0))
    return jnp.stack(history)[:, None]


def solution(mesh):
    return jax.shard_map(
        body,
        mesh=mesh,
        in_specs=(
            P("layer", "row", None, None),
            P("layer", "row", None),
            P(None, "layer", None, "row"),
            P("layer", None, "row"),
        ),
        out_specs=P(None, "layer", None, "row"),
        check_vma=False,
    )
```
